128 devices in a mesh: kv: 16 (over x, z), ep: 8 (over y, core).
Axes of the slice: x: 4, y: 4, z: 4, core: 2. Of those that a mesh axis runs over, the one named last changes fastest.
Arguments:
- queries: bfloat16 [64, 128, 576], P('ep'), may hold values from -64 to 64
- latent_cache: bfloat16 [64, 16384, 576], P('ep', 'kv'), may hold values from -7 to 7
- lengths: int32 [64], P('ep'), may hold values from 2 to 16384, as said below
- value_up: bfloat16 [128, 512, 128], P('kv'), may hold values from -6 to 6
- out_proj: bfloat16 [16384, 7168], P('kv', 'ep'), may hold values from -0.046875 to 0.046875
- residual: bfloat16 [64, 7168], P('kv', 'ep'), may hold values from -6 to 6
- norm_gain: float32 [7168], replicated, may hold values from 0.5 to 1.5
- route_ids: int32 [64, 8], replicated, may hold values from 0 to 15, all different within a row; in each aligned block of 64 rows (0 to 63, 64 to 127, ...) at most 48 rows name the same one
- route_gates: float32 [64, 8], replicated, may hold values from 0.1 to 1
- gate_weight: bfloat16 [16, 7168, 2048], P('kv', None, 'ep'), may hold values from -0.0625 to 0.0625
- up_weight: bfloat16 [16, 7168, 2048], P('kv', None, 'ep'), may hold values from -0.0625 to 0.0625
- down_weight: bfloat16 [16, 2048, 7168], P('kv', 'ep'), may hold values from -0.125 to 0.125
Outputs:
- attended: bfloat16 [64, 7168], P('kv', 'ep')
- expert_out: bfloat16 [64, 7168], P('kv', 'ep')
The draws below stay inside these ranges and needn't reach their ends.
Inputs may be any that keep to these rules, and one draw needn't show every extreme that they name: `lengths`: some row has the full length 16384. `route_ids`: the 8 experts of a row differ; no expert is chosen by more than 48 rows, a bound that some block reaches.
All inputs are finite; a program needn't handle non-finite values.
Results may differ from the reference program's by a relative error of at most 0.025.
Values may be sent and summed in bfloat16 or wider, within the bound.
No kernel may reach another device: no remote copies, remote signals or barrier semaphores. Data moves between devices by JAX's collectives and lax.ppermute only.
A program may use at most 128 MiB of HBM per device.

```python
import math
import jax
import jax.numpy as jnp
import numpy as np
from jax import lax

D = 7168
FF = 2048
HEADS = 128
LAT = 512
ROPE = 64
VHEAD = 128
TOP = 8
CTX_DEV = 1024
ROWS = 64
SEQ = 16384
EXPERTS = 16
CAP = 48
N_KV = 16


def draw_queries(key, part):
    key = jax.random.fold_in(key, 11)
    key_drawn = jax.random.fold_in(key, 0)
    drawn = jnp.clip(jax.random.normal(key_drawn, (ROWS, HEADS, LAT + ROPE), jnp.float32), -6.0, 6.0)
    return drawn.astype(jnp.bfloat16)


def draw_latent_cache(key, part):
    key = jax.random.fold_in(key, 12)
    key_drawn = jax.random.fold_in(key, 0)
    drawn = jnp.clip(jax.random.normal(key_drawn, (ROWS, SEQ, LAT + ROPE), jnp.float32), -6.0, 6.0)
    return drawn.astype(jnp.bfloat16)


def draw_lengths(key, part):
    key = jax.random.fold_in(key, 13)
    key_len, key_long = jax.random.split(key, 2)
    drawn_len = jax.random.randint(key_len, (ROWS,), 2, SEQ + 1)
    longest = jax.random.randint(key_long, (), 0, ROWS)
    return jnp.where(jnp.arange(ROWS) == longest, SEQ, drawn_len).astype(jnp.int32)


def shard_levels(own_key, extent, cuts, least, largest):
    loudness, own = 1.0, jax.random.fold_in(own_key, 6)
    for axis_at, shards_of in cuts:
        steps = jnp.exp(jax.random.uniform(jax.random.fold_in(own, axis_at), (shards_of,), jnp.float32, least / len(cuts), largest / len(cuts)))
        loudness = loudness * jnp.repeat(steps, extent[axis_at] // shards_of).reshape([-1 if axis == axis_at else 1 for axis in range(len(extent))])
    return loudness


def deal_out(key, own, number, rows, count, top, most, slope):
    sequence = jax.random.permutation(key, count)
    crowded, usual = portions_of(count, rows * top, most, slope, True), portions_of(count, rows * top, most, slope, False)
    places = jnp.arange(count)

    def named(sizes, turn):
        used = int((sizes > 0).sum())
        fixed = max(1, used // 4)
        passed = fixed + (places - fixed + turn * (used - fixed)) % max(1, count - fixed)
        return jnp.zeros((count,), jnp.int32).at[sequence[jnp.where(places < fixed, places, passed)]].set(jnp.asarray(sizes, jnp.int32))

    sizes = jnp.where(number % 4 == 0, named(crowded, number // 4), named(usual, number - number // 4 - 1))
    mixed = jax.random.permutation(jax.random.fold_in(own, 3), count)
    donor, sink = mixed[0:count // 2 * 2:2], mixed[1:count // 2 * 2:2]
    slack = jnp.minimum(sizes[donor] - 1, most - sizes[sink]) // 2
    slack = jnp.where((donor == sequence[0]) | (sink == sequence[0]) | (sizes[sink] == 0), 0, jnp.maximum(slack, 0))
    passed = jax.random.randint(jax.random.fold_in(own, 4), (count // 2,), 0, 1 << 20) % (slack + 1)
    sizes = sizes.at[donor].add(-passed).at[sink].add(passed)
    labels = jnp.searchsorted(jnp.cumsum(sizes), jnp.arange(rows * top), side="right").astype(jnp.int32)
    grid = labels.reshape(top, rows).T
    grid = grid[jax.random.permutation(jax.random.fold_in(own, 1), rows)]
    turn = jax.random.randint(jax.random.fold_in(own, 2), (rows, 1), 0, top)
    return jnp.take_along_axis(grid, (jnp.arange(top)[None, :] + turn) % top, axis=1)


def portions_of(number_of, total, reach, skew, full):
    loads = [(1 << 20) // math.isqrt(grade ** skew) + 1 for grade in range(1, number_of + 1)]
    largest = reach if full else min(reach, max(-(-total // number_of), total * loads[0] // sum(loads)))
    least = 1 if total - largest >= number_of - 1 else 0
    holding, spare = [largest] + [least] * (number_of - 1), total - largest - least * (number_of - 1)
    while spare > 0:
        movable = [i for i in range(1, number_of) if holding[i] < largest] or [i for i in range(1, number_of) if holding[i] < reach]
        pool, left = sum([loads[i] for i in movable]), spare
        for i in movable:
            extra = min(reach - holding[i], max(1, left * loads[i] // pool), spare)
            holding[i] = holding[i] + extra
            spare = spare - extra
    return np.array(holding)


def bell_draw(stream_key, extent, spread, most, pieces=(), kind=jnp.bfloat16):
    values = jax.random.normal(stream_key, extent, jnp.float32) * spread
    if len(pieces) > 0:
        values = shard_levels(stream_key, extent, pieces, -0.22, 0.18) * values
    return jnp.clip(values, min=-most, max=most).astype(kind)


def setup_inputs(seed: int = 0) -> dict:
    keys = jax.random.split(jax.random.key(seed), 13)
    queries = draw_queries(jax.random.fold_in(keys[12], 71), 0)
    latent_cache = draw_latent_cache(jax.random.fold_in(keys[12], 71), 0)
    lengths = draw_lengths(jax.random.fold_in(keys[12], 71), 0)
    value_up = bell_draw(keys[3], (HEADS, LAT, VHEAD), 1.0, 6.0, ((0, 16),))
    out_proj = bell_draw(keys[4], (HEADS * VHEAD, D), (HEADS * VHEAD) ** -0.5, 0.046875, ((0, 16), (1, 8)))
    residual = bell_draw(keys[5], (ROWS, D), 1.0, 6.0, ((0, 16), (1, 8)))
    norm_gain = jnp.clip(1.0 + 0.1 * jax.random.normal(keys[6], (D,), jnp.float32), 0.5, 1.5)
    route_ids_keys = jax.random.split(jax.random.fold_in(keys[7], 1), ROWS // ROWS)
    route_ids_turns = jax.random.permutation(jax.random.fold_in(keys[7], 3), ROWS // ROWS)
    route_ids = jax.vmap(lambda own, number: deal_out(jax.random.fold_in(keys[7], 2), own, number, ROWS, EXPERTS, TOP, CAP, 2))(route_ids_keys, route_ids_turns).reshape((ROWS, TOP))
    route_gates = jnp.clip(jnp.exp(jax.random.uniform(keys[8], (ROWS, TOP), jnp.float32, math.log(0.1), math.log(1.0))), 0.1, 1.0)
    gate_weight = bell_draw(keys[9], (EXPERTS, D, FF), D ** -0.5, 0.0625, ((0, 16), (2, 8)))
    up_weight = bell_draw(keys[10], (EXPERTS, D, FF), D ** -0.5, 0.0625, ((0, 16), (2, 8)))
    down_weight = bell_draw(keys[11], (EXPERTS, FF, D), FF ** -0.5, 0.125, ((0, 16), (1, 8)))
    return {"queries": queries, "latent_cache": latent_cache, "lengths": lengths, "value_up": value_up, "out_proj": out_proj, "residual": residual, "norm_gain": norm_gain, "route_ids": route_ids, "route_gates": route_gates, "gate_weight": gate_weight, "up_weight": up_weight, "down_weight": down_weight}


SCORE_SCALE = 0.07216878364870323
NEG_FILL = -1e+30
NORM_EPS = 1e-06

def attend_row(packed):
    query_row, cache_row, row_length = packed
    scores = jnp.dot(query_row, cache_row.T, preferred_element_type=jnp.float32) * SCORE_SCALE
    scores = scores.reshape(HEADS, N_KV, CTX_DEV)
    position = jnp.arange(SEQ, dtype=jnp.int32).reshape(N_KV, CTX_DEV)
    allowed = (position < row_length)[None, :, :]
    masked = jnp.where(allowed, scores, NEG_FILL)
    block_max = lax.optimization_barrier(jnp.max(masked, axis=2))
    exp_terms = jnp.where(allowed, jnp.exp(masked - block_max[:, :, None]), 0.0)
    block_sum = lax.optimization_barrier(jnp.sum(exp_terms, axis=2))
    latents = cache_row[:, :LAT].reshape(N_KV, CTX_DEV, LAT).astype(jnp.float32)
    block_out = jnp.einsum('hkt,ktc->hkc', exp_terms.astype(jnp.bfloat16).astype(jnp.float32), latents)
    highest = lax.optimization_barrier(jnp.max(block_max, axis=1))
    factor = jnp.exp(block_max - highest[:, None])
    denominator = lax.optimization_barrier(jnp.sum(factor * block_sum, axis=1))
    merged = lax.optimization_barrier(jnp.sum(factor[:, :, None] * block_out, axis=1)) / denominator[:, None]
    return merged.astype(jnp.bfloat16)

def reference(queries, latent_cache, lengths, value_up, out_proj, residual, norm_gain, route_ids, route_gates, gate_weight, up_weight, down_weight):
    attention = lax.map(attend_row, (queries, latent_cache, lengths))
    head_values = jnp.einsum('bhc,hcv->bhv', attention.astype(jnp.float32), value_up.astype(jnp.float32))
    head_values = head_values.astype(jnp.bfloat16).reshape(ROWS, HEADS * VHEAD)
    projected = jnp.dot(head_values, out_proj, preferred_element_type=jnp.float32)
    attended = (residual.astype(jnp.float32) + projected).astype(jnp.bfloat16)
    attended_wide = attended.astype(jnp.float32)
    inverse = lax.rsqrt(lax.optimization_barrier(jnp.mean(attended_wide * attended_wide, axis=1)) + NORM_EPS)
    normed = (attended_wide * inverse[:, None] * norm_gain[None, :]).astype(jnp.bfloat16)

    def expert_term(running, expert_index):
        gate_act = jnp.dot(normed, gate_weight[expert_index], preferred_element_type=jnp.float32)
        up_act = jnp.dot(normed, up_weight[expert_index], preferred_element_type=jnp.float32)
        hidden = (jax.nn.silu(gate_act) * up_act).astype(jnp.bfloat16)
        produced = jnp.dot(hidden, down_weight[expert_index], preferred_element_type=jnp.float32)
        chosen = (route_ids == expert_index).astype(jnp.float32)
        row_gate = lax.optimization_barrier(jnp.sum(chosen * route_gates, axis=1))
        return (running + produced * row_gate[:, None], None)
    started = jnp.zeros((ROWS, D), jnp.float32)
    summed, unused = lax.scan(expert_term, started, jnp.arange(EXPERTS, dtype=jnp.int32))
    return (attended, summed.astype(jnp.bfloat16))
```

```python
import functools

import jax
import jax.numpy as jnp
from jax import lax
from jax.experimental import pallas as pl
from jax.experimental.pallas import tpu as pltpu
from jax.sharding import PartitionSpec as P

SCORE_SCALE = 0.07216878364870323
LOG2_E = 1.4426950408889634
NEG_FILL = -1e30
NORM_EPS = 1e-06
EXTRA = 128
MIB = 1 << 20


def split_three(value):
    high = value.astype(jnp.bfloat16).astype(jnp.float32)
    rest = value - high
    mid = rest.astype(jnp.bfloat16).astype(jnp.float32)
    return high, mid, rest - mid


def attention_kernel(lengths_ref, q_hbm, cache_hbm, out_ref, q_ref, cache_ref, arrived):
    row_count, unused_width, ctx_len = cache_ref.shape
    head_count = q_ref.shape[2]
    groups = out_ref.shape[0]
    lat_width = out_ref.shape[2] - EXTRA
    per_group = head_count // groups

    start = lax.axis_index("kv") * ctx_len

    def fetch(row):
        return (
            pltpu.make_async_copy(q_hbm.at[row], q_ref.at[row], arrived.at[0, row]),
            pltpu.make_async_copy(cache_hbm.at[row], cache_ref.at[row], arrived.at[1, row]),
        )

    for row in range(row_count):
        for copy in fetch(row):
            copy.start()
    lane = lax.broadcasted_iota(jnp.int32, (head_count, EXTRA), 1)
    position = lax.broadcasted_iota(jnp.int32, (head_count, ctx_len), 1)
    for pair in range(0, row_count, 2):
        outs = []
        extras = []
        for row in (pair, pair + 1):
            for copy in fetch(row):
                copy.wait()
            scores = lax.dot_general(
                q_ref[row],
                cache_ref[row],
                (((0,), (0,)), ((), ())),
                preferred_element_type=jnp.float32,
            )
            scores = jnp.where(
                position < lengths_ref[row] - start, scores * (SCORE_SCALE * LOG2_E), NEG_FILL
            )
            top = jnp.max(scores, axis=1, keepdims=True)
            terms = jnp.exp2(scores - top)
            total = jnp.sum(terms, axis=1, keepdims=True)
            out = lax.dot_general(
                terms.astype(jnp.bfloat16),
                cache_ref[row, :lat_width, :],
                (((1,), (1,)), ((), ())),
                preferred_element_type=jnp.float32,
            )
            extra = jnp.zeros((head_count, EXTRA), jnp.float32)
            for at, piece in enumerate(split_three(top) + split_three(total)):
                extra = jnp.where(lane == at, piece, extra)
            outs.append(out.reshape(groups, per_group, lat_width))
            extras.append(extra.reshape(groups, per_group, EXTRA))
        spot = slice(pair * per_group, (pair + 2) * per_group)
        out_ref[:, spot, :lat_width] = jnp.concatenate(outs, axis=1).astype(jnp.bfloat16)
        out_ref[:, spot, lat_width:] = jnp.concatenate(extras, axis=1).astype(jnp.bfloat16)


def attend_block(lengths, queries, latent_cache, groups, lat_width):
    row_count, width, ctx_len = latent_cache.shape
    head_count = queries.shape[2]
    pairs = row_count * (head_count // groups)
    return pl.pallas_call(
        attention_kernel,
        in_specs=[
            pl.BlockSpec(memory_space=pltpu.SMEM),
            pl.BlockSpec(memory_space=pltpu.HBM),
            pl.BlockSpec(memory_space=pltpu.HBM),
        ],
        out_specs=pl.BlockSpec(memory_space=pltpu.VMEM),
        out_shape=jax.ShapeDtypeStruct((groups, pairs, lat_width + EXTRA), jnp.bfloat16),
        scratch_shapes=[
            pltpu.VMEM((row_count, width, head_count), jnp.bfloat16),
            pltpu.VMEM((row_count, width, ctx_len), jnp.bfloat16),
            pltpu.SemaphoreType.DMA((2, row_count)),
        ],
        compiler_params=pltpu.CompilerParams(vmem_limit_bytes=54 * MIB),
        cost_estimate=pl.CostEstimate(
            flops=2 * row_count * head_count * ctx_len * (width + lat_width),
            bytes_accessed=2 * latent_cache.size + 2 * queries.size,
            transcendentals=row_count * head_count * ctx_len,
        ),
        name="attend_block",
    )(lengths, queries, latent_cache)


def merge_kernel(parts_ref, value_ref, out_ref, merged_ref):
    block_count, pairs, wide = parts_ref.shape
    heads, lat_width, value_width = value_ref.shape
    rows = pairs // heads
    extra = parts_ref[:, :, lat_width:].astype(jnp.float32)
    top = extra[:, :, 0:1] + extra[:, :, 1:2] + extra[:, :, 2:3]
    total = extra[:, :, 3:4] + extra[:, :, 4:5] + extra[:, :, 5:6]
    factor = jnp.exp2(top - jnp.max(top, axis=0, keepdims=True))
    denominator = jnp.sum(factor * total, axis=0)
    merged = jnp.zeros((pairs, lat_width), jnp.float32)
    for k in range(block_count):
        merged = merged + factor[k] * parts_ref[k, :, :lat_width].astype(jnp.float32)
    merged = merged / denominator
    tiles = merged_ref.shape[0]
    for t in range(tiles):
        merged_ref[t] = merged[:, t * EXTRA : (t + 1) * EXTRA]
    copies = out_ref.shape[0] // rows
    for h in range(heads):
        attention = jnp.concatenate(
            [merged_ref[t, pl.ds(h, rows, stride=heads), :] for t in range(tiles)], axis=1
        ).astype(jnp.bfloat16)
        value = jnp.dot(attention, value_ref[h], preferred_element_type=jnp.float32)
        out_ref[:, h * value_width : (h + 1) * value_width] = jnp.concatenate(
            [value] * copies, axis=0
        ).astype(jnp.bfloat16)


def merge_blocks(parts, value_up, copies):
    heads, lat_width, value_width = value_up.shape
    pairs = parts.shape[1]
    return pl.pallas_call(
        merge_kernel,
        out_shape=jax.ShapeDtypeStruct(
            (copies * (pairs // heads), heads * value_width), jnp.bfloat16
        ),
        scratch_shapes=[pltpu.VMEM((lat_width // EXTRA, pairs, EXTRA), jnp.float32)],
        compiler_params=pltpu.CompilerParams(vmem_limit_bytes=32 * MIB),
        name="merge_blocks",
    )(parts, value_up)


def residual_kernel(parts_ref, residual_ref, attended_ref, spread_ref):
    total = residual_ref[...].astype(jnp.float32)
    for k in range(parts_ref.shape[0]):
        total = total + parts_ref[k].astype(jnp.float32)
    attended = total.astype(jnp.bfloat16)
    attended_ref[...] = attended
    for i in range(spread_ref.shape[0]):
        spread_ref[i] = attended


def add_residual(parts, residual, copies):
    return pl.pallas_call(
        residual_kernel,
        out_shape=(
            jax.ShapeDtypeStruct(residual.shape, jnp.bfloat16),
            jax.ShapeDtypeStruct((copies,) + residual.shape, jnp.bfloat16),
        ),
        compiler_params=pltpu.CompilerParams(vmem_limit_bytes=8 * MIB),
        cost_estimate=pl.CostEstimate(
            flops=parts.size, bytes_accessed=2 * (copies * residual.size), transcendentals=0
        ),
        name="add_residual",
    )(parts, residual)


def expert_kernel(
    mine_ref,
    other_ref,
    gain_ref,
    ids_ref,
    gates_ref,
    w_gate_hbm,
    w_up_hbm,
    w_down_hbm,
    keep_ref,
    give_ref,
    normed_ref,
    w_gate_ref,
    w_up_ref,
    w_down_ref,
    arrived,
):
    chips, row_count, col_count = mine_ref.shape
    full_width = normed_ref.shape[1]
    part = full_width // chips

    def span(y):
        return slice(y * part, (y + 1) * part)

    def fetch_in(y):
        at = span(y)
        return (
            pltpu.make_async_copy(w_gate_hbm.at[at], w_gate_ref.at[at], arrived.at[0, y]),
            pltpu.make_async_copy(w_up_hbm.at[at], w_up_ref.at[at], arrived.at[1, y]),
        )

    def fetch_out(y):
        at = span(y)
        return pltpu.make_async_copy(
            w_down_hbm.at[:, at], w_down_ref.at[:, at], arrived.at[2, y]
        )

    for y in range(chips):
        for copy in fetch_in(y):
            copy.start()
    for y in range(chips):
        fetch_out(y).start()

    expert = lax.axis_index("kv")
    first = lax.rem(lax.axis_index("ep"), 2) == 0
    squares = jnp.zeros((row_count, col_count), jnp.float32)
    for y in range(chips):
        for piece in (mine_ref[y], other_ref[y]):
            wide = piece.astype(jnp.float32)
            squares = squares + wide * wide
    inverse = lax.rsqrt(jnp.sum(squares, axis=1, keepdims=True) / full_width + NORM_EPS)
    chosen = jnp.where(ids_ref[...] == expert, gates_ref[...], 0.0)
    in_lanes = jnp.sum(chosen, axis=0, keepdims=True)
    square = (row_count, row_count)
    same = lax.broadcasted_iota(jnp.int32, square, 0) == lax.broadcasted_iota(
        jnp.int32, square, 1
    )
    row_gate = jnp.sum(jnp.where(same, in_lanes, 0.0), axis=1, keepdims=True)
    gate_act = jnp.zeros((row_count, w_gate_ref.shape[1]), jnp.float32)
    up_act = gate_act
    for y in range(chips):
        mine = mine_ref[y].astype(jnp.float32)
        other = other_ref[y].astype(jnp.float32)
        for c, piece in enumerate(
            (jnp.where(first, mine, other), jnp.where(first, other, mine))
        ):
            cols = slice((2 * y + c) * col_count, (2 * y + c + 1) * col_count)
            normed_ref[:, cols] = (piece * inverse * gain_ref[:, cols]).astype(jnp.bfloat16)
        for copy in fetch_in(y):
            copy.wait()
        normed = normed_ref[:, span(y)]
        gate_act = gate_act + jnp.dot(
            normed, w_gate_ref[span(y)], preferred_element_type=jnp.float32
        )
        up_act = up_act + jnp.dot(
            normed, w_up_ref[span(y)], preferred_element_type=jnp.float32
        )
    hidden = (gate_act / (1.0 + jnp.exp(-gate_act)) * up_act).astype(jnp.bfloat16)
    for y in range(chips):
        fetch_out(y).wait()
        both = [
            jnp.dot(
                hidden,
                w_down_ref[:, (2 * y + c) * col_count : (2 * y + c + 1) * col_count],
                preferred_element_type=jnp.float32,
            )
            * row_gate
            for c in range(2)
        ]
        keep_ref[y] = jnp.where(first, both[0], both[1]).astype(jnp.bfloat16)
        give_ref[y] = jnp.where(first, both[1], both[0]).astype(jnp.bfloat16)


def run_expert(mine, other, gain, ids, gates, w_gate, w_up, w_down):
    chips, row_count, unused_cols = mine.shape
    full_width, hidden_width = w_gate.shape
    vmem = pl.BlockSpec(memory_space=pltpu.VMEM)
    hbm = pl.BlockSpec(memory_space=pltpu.HBM)
    half = jax.ShapeDtypeStruct(mine.shape, jnp.bfloat16)
    return pl.pallas_call(
        expert_kernel,
        in_specs=[vmem] * 5 + [hbm] * 3,
        out_specs=(vmem, vmem),
        out_shape=(half, half),
        scratch_shapes=[
            pltpu.VMEM((row_count, full_width), jnp.bfloat16),
            pltpu.VMEM(w_gate.shape, jnp.bfloat16),
            pltpu.VMEM(w_up.shape, jnp.bfloat16),
            pltpu.VMEM(w_down.shape, jnp.bfloat16),
            pltpu.SemaphoreType.DMA((3, chips)),
        ],
        compiler_params=pltpu.CompilerParams(vmem_limit_bytes=54 * MIB),
        cost_estimate=pl.CostEstimate(
            flops=6 * row_count * full_width * hidden_width,
            bytes_accessed=6 * full_width * hidden_width,
            transcendentals=row_count * hidden_width,
        ),
        name="run_expert",
    )(mine, other, gain, ids, gates, w_gate, w_up, w_down)


def pair_kernel(keep_ref, given_ref, out_ref):
    chips, row_count, unused_cols = keep_ref.shape
    own_rows = out_ref.shape[1]
    for y in range(chips):
        both = keep_ref[y].astype(jnp.float32) + given_ref[y].astype(jnp.float32)
        for k in range(row_count // own_rows):
            out_ref[y * (row_count // own_rows) + k] = both[
                k * own_rows : (k + 1) * own_rows
            ].astype(jnp.bfloat16)


def add_pair(keep, given, own_rows):
    chips, row_count, col_count = keep.shape
    return pl.pallas_call(
        pair_kernel,
        out_shape=jax.ShapeDtypeStruct(
            (chips * row_count // own_rows, own_rows, col_count), jnp.bfloat16
        ),
        compiler_params=pltpu.CompilerParams(vmem_limit_bytes=8 * MIB),
        cost_estimate=pl.CostEstimate(
            flops=keep.size, bytes_accessed=6 * keep.size, transcendentals=0
        ),
        name="add_pair",
    )(keep, given)


def total_kernel(parts_ref, out_ref):
    total = parts_ref[0].astype(jnp.float32)
    for k in range(1, parts_ref.shape[0]):
        total = total + parts_ref[k].astype(jnp.float32)
    out_ref[...] = total.astype(jnp.bfloat16)


def add_total(parts):
    return pl.pallas_call(
        total_kernel,
        out_shape=jax.ShapeDtypeStruct(parts.shape[1:], jnp.bfloat16),
        compiler_params=pltpu.CompilerParams(vmem_limit_bytes=8 * MIB),
        name="add_total",
    )(parts)


def on_device(
    queries,
    latent_cache,
    lengths,
    value_up,
    out_proj,
    residual,
    norm_gain,
    route_ids,
    route_gates,
    gate_weight,
    up_weight,
    down_weight,
):
    kv_count = lax.axis_size("kv")
    ep_count = lax.axis_size("ep")
    chips = ep_count // 2
    both = ("kv", "ep")
    same_core = [
        [kv * ep_count + y * 2 + c for y in range(chips) for kv in range(kv_count)]
        for c in range(2)
    ]
    other_core = [(i, i ^ 1) for i in range(ep_count)]
    lat_width = value_up.shape[1]

    parts = attend_block(
        lengths,
        jnp.swapaxes(queries, 1, 2),
        jnp.swapaxes(latent_cache, 1, 2),
        kv_count,
        lat_width,
    )
    parts = lax.all_to_all(parts, "kv", split_axis=0, concat_axis=0, tiled=True)
    head_values = merge_blocks(parts, value_up, ep_count)
    all_values = lax.all_to_all(head_values, "ep", split_axis=0, concat_axis=0, tiled=True)
    row_count = all_values.shape[0]
    col_count = out_proj.shape[1]
    own_rows = row_count // kv_count
    projected = jnp.dot(all_values, out_proj, preferred_element_type=jnp.float32)
    projected = projected.astype(jnp.bfloat16).reshape(kv_count, own_rows, col_count)
    projected = lax.all_to_all(projected, "kv", split_axis=0, concat_axis=0, tiled=True)
    attended, spread = add_residual(projected, residual, kv_count * chips)

    mine = lax.all_to_all(
        spread, both, split_axis=0, concat_axis=0, tiled=True, axis_index_groups=same_core
    ).reshape(chips, row_count, col_count)
    other = lax.ppermute(mine, "ep", other_core)
    keep, give = run_expert(
        mine,
        other,
        norm_gain[None],
        route_ids.T,
        route_gates.T,
        gate_weight[0],
        up_weight[0],
        down_weight[0],
    )
    given = lax.ppermute(give, "ep", other_core)
    summed = add_pair(keep, given, own_rows)
    arrived = lax.all_to_all(
        summed, both, split_axis=0, concat_axis=0, tiled=True, axis_index_groups=same_core
    )
    return (attended, add_total(arrived))


def solution(mesh):
    return jax.shard_map(
        on_device,
        mesh=mesh,
        in_specs=(
            P("ep", None, None),
            P("ep", "kv", None),
            P("ep"),
            P("kv", None, None),
            P("kv", "ep"),
            P("kv", "ep"),
            P(),
            P(),
            P(),
            P("kv", None, "ep"),
            P("kv", None, "ep"),
            P("kv", "ep", None),
        ),
        out_specs=(P("kv", "ep"), P("kv", "ep")),
        check_vma=False,
    )
```

```python
import functools

import jax
import jax.numpy as jnp
from jax import lax
from jax.experimental import pallas as pl
from jax.experimental.pallas import tpu as pltpu
from jax.sharding import PartitionSpec as P

SCORE_SCALE = 0.07216878364870323
LOG2_E = 1.4426950408889634
NEG_FILL = -1e30
NORM_EPS = 1e-06
LANES = 128
MIB = 1 << 20


def in_hbm(array):
    return pltpu.with_memory_space_constraint(array, pltpu.HBM)


def split_three(value):
    high = value.astype(jnp.bfloat16).astype(jnp.float32)
    rest = value - high
    mid = rest.astype(jnp.bfloat16).astype(jnp.float32)
    return high, mid, rest - mid


def attention_kernel(lengths_ref, q_hbm, cache_hbm, *refs):
    weight_count = (len(refs) - 4) // 2
    weights_hbm = refs[:weight_count]
    out_ref = refs[weight_count]
    weights_ref = refs[weight_count + 1 : -3]
    q_ref, cache_ref, arrived = refs[-3:]
    row_count, unused_width, ctx_len = cache_ref.shape
    head_count = q_ref.shape[2]
    groups = out_ref.shape[0]
    lat_width = out_ref.shape[2]
    per_group = head_count // groups
    start = lax.axis_index("kv") * ctx_len

    def fetch(row):
        return (
            pltpu.make_async_copy(q_hbm.at[row], q_ref.at[row], arrived.at[0, row]),
            pltpu.make_async_copy(cache_hbm.at[row], cache_ref.at[row], arrived.at[1, row]),
        )

    extra_copies = [
        pltpu.make_async_copy(weights_hbm[i], weights_ref[i], arrived.at[2, i])
        for i in range(weight_count)
    ]
    for row in range(row_count):
        for copy in fetch(row):
            copy.start()
    for copy in extra_copies:
        copy.start()
    position = lax.broadcasted_iota(jnp.int32, (head_count, ctx_len), 1)
    square = (head_count, head_count)
    same = lax.broadcasted_iota(jnp.int32, square, 0) == lax.broadcasted_iota(
        jnp.int32, square, 1
    )
    line = lax.broadcasted_iota(jnp.int32, (row_count, head_count), 0)
    levels = jnp.zeros((row_count, head_count), jnp.float32)
    for pair in range(0, row_count, 2):
        rows = (pair, pair + 1)
        for row in rows:
            for copy in fetch(row):
                copy.wait()
        scores = [
            lax.dot_general(
                q_ref[row],
                cache_ref[row],
                (((0,), (0,)), ((), ())),
                preferred_element_type=jnp.float32,
            )
            for row in rows
        ]
        scores = [
            jnp.where(position < lengths_ref[row] - start, s * (SCORE_SCALE * LOG2_E), NEG_FILL)
            for row, s in zip(rows, scores)
        ]
        tops = [jnp.max(s, axis=1, keepdims=True) for s in scores]
        terms = [jnp.exp2(s - top) for s, top in zip(scores, tops)]
        totals = [jnp.sum(t, axis=1, keepdims=True) for t in terms]
        outs = [
            lax.dot_general(
                t.astype(jnp.bfloat16),
                cache_ref[row, :lat_width, :],
                (((1,), (1,)), ((), ())),
                preferred_element_type=jnp.float32,
            )
            for row, t in zip(rows, terms)
        ]
        outs = [
            (o * (1.0 / total)).reshape(groups, per_group, lat_width)
            for o, total in zip(outs, totals)
        ]
        spot = slice(pair * per_group, (pair + 2) * per_group)
        out_ref[:, spot, :] = jnp.concatenate(outs, axis=1).astype(jnp.bfloat16)
        for row, top, total in zip(rows, tops, totals):
            level = jnp.sum(
                jnp.where(same, top + jnp.log2(total), 0.0), axis=0, keepdims=True
            )
            levels = jnp.where(line == row, level, levels)
    blank = jnp.zeros((row_count, lat_width - 3 * head_count), jnp.float32)
    stats = jnp.concatenate(split_three(levels) + (blank,), axis=1).astype(jnp.bfloat16)
    for k in range(groups):
        out_ref[k, row_count * per_group :, :] = stats
    for copy in extra_copies:
        copy.wait()


def attend_block(lengths, queries, latent_cache, groups, lat_width, weights):
    row_count, width, ctx_len = latent_cache.shape
    head_count = queries.shape[2]
    pairs = row_count * (head_count // groups)
    hbm = pl.BlockSpec(memory_space=pltpu.HBM)
    vmem = pl.BlockSpec(memory_space=pltpu.VMEM)
    return pl.pallas_call(
        attention_kernel,
        in_specs=[pl.BlockSpec(memory_space=pltpu.SMEM)] + [hbm] * (2 + len(weights)),
        out_specs=[vmem] * (1 + len(weights)),
        out_shape=[jax.ShapeDtypeStruct((groups, pairs + row_count, lat_width), jnp.bfloat16)]
        + [pltpu.VMEM(w.shape, w.dtype) for w in weights],
        scratch_shapes=[
            pltpu.VMEM((row_count, width, head_count), jnp.bfloat16),
            pltpu.VMEM((row_count, width, ctx_len), jnp.bfloat16),
            pltpu.SemaphoreType.DMA((3, row_count)),
        ],
        compiler_params=pltpu.CompilerParams(vmem_limit_bytes=28 * MIB),
        cost_estimate=pl.CostEstimate(
            flops=2 * row_count * head_count * ctx_len * (width + lat_width),
            bytes_accessed=2 * latent_cache.size + 2 * queries.size,
            transcendentals=row_count * head_count * ctx_len,
        ),
        name="attend_block",
    )(in_hbm(lengths), in_hbm(queries), in_hbm(latent_cache), *(in_hbm(w) for w in weights))


def merge_kernel(parts_ref, value_ref, *refs):
    out_ref, merged_ref = refs[-2:]
    block_count = parts_ref.shape[0]
    heads, lat_width, value_width = value_ref.shape
    rows = parts_ref.shape[1] // (heads + 1)
    pairs = rows * heads
    lanes = heads * block_count
    stats = parts_ref[:, pairs:, :].astype(jnp.float32)
    levels = (
        stats[:, :, :lanes] + stats[:, :, lanes : 2 * lanes] + stats[:, :, 2 * lanes : 3 * lanes]
    )
    factor = jnp.exp2(levels - jnp.max(levels, axis=0, keepdims=True))
    factor = factor / jnp.sum(factor, axis=0, keepdims=True)
    shape = (rows, heads, lanes)
    own = lax.broadcasted_iota(jnp.int32, shape, 2) == lax.broadcasted_iota(
        jnp.int32, shape, 1
    ) + heads * lax.axis_index("kv")
    merged = jnp.zeros((pairs, lat_width), jnp.float32)
    for k in range(block_count):
        column = jnp.sum(jnp.where(own, factor[k][:, None, :], 0.0), axis=2, keepdims=True)
        merged = merged + column.reshape(pairs, 1) * parts_ref[k, :pairs, :].astype(jnp.float32)
    tiles = merged_ref.shape[0]
    for t in range(tiles):
        merged_ref[t] = merged[:, t * LANES : (t + 1) * LANES]
    copies = out_ref.shape[0] // rows
    for h in range(heads):
        attention = jnp.concatenate(
            [merged_ref[t, pl.ds(h, rows, stride=heads), :] for t in range(tiles)], axis=1
        ).astype(jnp.bfloat16)
        value = jnp.dot(attention, value_ref[h], preferred_element_type=jnp.float32)
        out_ref[:, h * value_width : (h + 1) * value_width] = jnp.concatenate(
            [value] * copies, axis=0
        ).astype(jnp.bfloat16)


def merge_blocks(parts, value_up, copies, held):
    heads, lat_width, value_width = value_up.shape
    pairs = parts.shape[1] // (heads + 1) * heads
    return pl.pallas_call(
        merge_kernel,
        out_shape=jax.ShapeDtypeStruct(
            (copies * (pairs // heads), heads * value_width), jnp.bfloat16
        ),
        scratch_shapes=[pltpu.VMEM((lat_width // LANES, pairs, LANES), jnp.float32)],
        compiler_params=pltpu.CompilerParams(vmem_limit_bytes=12 * MIB),
        name="merge_blocks",
    )(parts, value_up, *held)


def project_kernel(values_ref, proj_ref, *refs):
    out_ref = refs[-1]
    own_rows = out_ref.shape[1]
    projected = jnp.dot(values_ref[...], proj_ref[...], preferred_element_type=jnp.float32)
    for k in range(out_ref.shape[0]):
        out_ref[k] = projected[k * own_rows : (k + 1) * own_rows].astype(jnp.bfloat16)


def project(values, proj, groups, held):
    rows = values.shape[0]
    cols = proj.shape[1]
    return pl.pallas_call(
        project_kernel,
        out_shape=jax.ShapeDtypeStruct((groups, rows // groups, cols), jnp.bfloat16),
        compiler_params=pltpu.CompilerParams(vmem_limit_bytes=12 * MIB),
        cost_estimate=pl.CostEstimate(
            flops=2 * rows * proj.size, bytes_accessed=2 * proj.size, transcendentals=0
        ),
        name="project",
    )(values, proj, *held)


def residual_kernel(parts_ref, residual_ref, *refs):
    attended_ref, spread_ref = refs[-2:]
    total = residual_ref[...].astype(jnp.float32)
    for k in range(parts_ref.shape[0]):
        total = total + parts_ref[k].astype(jnp.float32)
    attended = total.astype(jnp.bfloat16)
    attended_ref[...] = attended
    for i in range(spread_ref.shape[0]):
        spread_ref[i] = attended


def add_residual(parts, residual, copies, held):
    return pl.pallas_call(
        residual_kernel,
        out_shape=(
            jax.ShapeDtypeStruct(residual.shape, jnp.bfloat16),
            jax.ShapeDtypeStruct((copies,) + residual.shape, jnp.bfloat16),
        ),
        compiler_params=pltpu.CompilerParams(vmem_limit_bytes=8 * MIB),
        cost_estimate=pl.CostEstimate(
            flops=parts.size, bytes_accessed=2 * copies * residual.size, transcendentals=0
        ),
        name="add_residual",
    )(parts, residual, *held)


def expert_kernel(
    mine_ref,
    other_ref,
    gain_ref,
    ids_ref,
    gates_ref,
    w_gate_ref,
    w_up_ref,
    w_down_ref,
    keep_ref,
    give_ref,
    normed_ref,
):
    chips, row_count, col_count = mine_ref.shape
    full_width = normed_ref.shape[1]
    expert = lax.axis_index("kv")
    first = lax.rem(lax.axis_index("ep"), 2) == 0
    squares = jnp.zeros((row_count, col_count), jnp.float32)
    for y in range(chips):
        for piece in (mine_ref[y], other_ref[y]):
            wide = piece.astype(jnp.float32)
            squares = squares + wide * wide
    inverse = lax.rsqrt(jnp.sum(squares, axis=1, keepdims=True) / full_width + NORM_EPS)
    chosen = jnp.where(ids_ref[...] == expert, gates_ref[...], 0.0)
    in_lanes = jnp.sum(chosen, axis=0, keepdims=True)
    square = (row_count, row_count)
    same = lax.broadcasted_iota(jnp.int32, square, 0) == lax.broadcasted_iota(
        jnp.int32, square, 1
    )
    row_gate = jnp.sum(jnp.where(same, in_lanes, 0.0), axis=1, keepdims=True)
    for y in range(chips):
        mine = mine_ref[y].astype(jnp.float32)
        other = other_ref[y].astype(jnp.float32)
        for c, piece in enumerate(
            (jnp.where(first, mine, other), jnp.where(first, other, mine))
        ):
            cols = slice((2 * y + c) * col_count, (2 * y + c + 1) * col_count)
            normed_ref[:, cols] = (piece * inverse * gain_ref[:, cols]).astype(jnp.bfloat16)
    normed = normed_ref[...]
    gate_act = jnp.dot(normed, w_gate_ref[...], preferred_element_type=jnp.float32)
    up_act = jnp.dot(normed, w_up_ref[...], preferred_element_type=jnp.float32)
    hidden = (gate_act / (1.0 + jnp.exp(-gate_act)) * up_act).astype(jnp.bfloat16)
    for y in range(chips):
        both = [
            jnp.dot(
                hidden,
                w_down_ref[:, (2 * y + c) * col_count : (2 * y + c + 1) * col_count],
                preferred_element_type=jnp.float32,
            )
            * row_gate
            for c in range(2)
        ]
        keep_ref[y] = jnp.where(first, both[0], both[1]).astype(jnp.bfloat16)
        give_ref[y] = jnp.where(first, both[1], both[0]).astype(jnp.bfloat16)


def run_expert(mine, other, gain, ids, gates, w_gate, w_up, w_down):
    row_count = mine.shape[1]
    full_width, hidden_width = w_gate.shape
    vmem = pl.BlockSpec(memory_space=pltpu.VMEM)
    half = jax.ShapeDtypeStruct(mine.shape, jnp.bfloat16)
    return pl.pallas_call(
        expert_kernel,
        in_specs=[vmem] * 8,
        out_specs=(vmem, vmem),
        out_shape=(half, half),
        scratch_shapes=[pltpu.VMEM((row_count, full_width), jnp.bfloat16)],
        compiler_params=pltpu.CompilerParams(vmem_limit_bytes=12 * MIB),
        cost_estimate=pl.CostEstimate(
            flops=6 * row_count * full_width * hidden_width,
            bytes_accessed=6 * full_width * hidden_width,
            transcendentals=row_count * hidden_width,
        ),
        name="run_expert",
    )(mine, other, gain, ids, gates, w_gate, w_up, w_down)


def pair_kernel(keep_ref, given_ref, out_ref):
    chips, row_count, unused_cols = keep_ref.shape
    own_rows = out_ref.shape[1]
    for y in range(chips):
        both = keep_ref[y].astype(jnp.float32) + given_ref[y].astype(jnp.float32)
        for k in range(row_count // own_rows):
            out_ref[y * (row_count // own_rows) + k] = both[
                k * own_rows : (k + 1) * own_rows
            ].astype(jnp.bfloat16)


def add_pair(keep, given, own_rows):
    chips, row_count, col_count = keep.shape
    return pl.pallas_call(
        pair_kernel,
        out_shape=jax.ShapeDtypeStruct(
            (chips * row_count // own_rows, own_rows, col_count), jnp.bfloat16
        ),
        compiler_params=pltpu.CompilerParams(vmem_limit_bytes=8 * MIB),
        cost_estimate=pl.CostEstimate(
            flops=keep.size, bytes_accessed=6 * keep.size, transcendentals=0
        ),
        name="add_pair",
    )(keep, given)


def total_kernel(parts_ref, out_ref):
    total = parts_ref[0].astype(jnp.float32)
    for k in range(1, parts_ref.shape[0]):
        total = total + parts_ref[k].astype(jnp.float32)
    out_ref[...] = total.astype(jnp.bfloat16)


def regroup_kernel(parts_ref, *refs):
    out_ref = refs[-1]
    chips = out_ref.shape[0]
    each = parts_ref.shape[0] // chips
    for y in range(chips):
        out_ref[y] = jnp.concatenate(
            [parts_ref[y * each + k].astype(jnp.float32) for k in range(each)], axis=0
        ).astype(jnp.bfloat16)


def regroup(parts, chips, held):
    count, rows, cols = parts.shape
    return pl.pallas_call(
        regroup_kernel,
        out_shape=jax.ShapeDtypeStruct((chips, count // chips * rows, cols), jnp.bfloat16),
        compiler_params=pltpu.CompilerParams(vmem_limit_bytes=8 * MIB),
        name="regroup",
    )(parts, *held)


def add_total(parts):
    return pl.pallas_call(
        total_kernel,
        out_shape=jax.ShapeDtypeStruct(parts.shape[1:], jnp.bfloat16),
        compiler_params=pltpu.CompilerParams(vmem_limit_bytes=8 * MIB),
        name="add_total",
    )(parts)


def on_device(
    queries,
    latent_cache,
    lengths,
    value_up,
    out_proj,
    residual,
    norm_gain,
    route_ids,
    route_gates,
    gate_weight,
    up_weight,
    down_weight,
):
    kv_count = lax.axis_size("kv")
    ep_count = lax.axis_size("ep")
    chips = ep_count // 2
    both = ("kv", "ep")
    same_core = [
        [kv * ep_count + y * 2 + c for y in range(chips) for kv in range(kv_count)]
        for c in range(2)
    ]
    other_core = [(i, i ^ 1) for i in range(ep_count)]
    lat_width = value_up.shape[1]

    parts, *weights = attend_block(
        lengths,
        jnp.swapaxes(queries, 1, 2),
        jnp.swapaxes(latent_cache, 1, 2),
        kv_count,
        lat_width,
        (gate_weight[0], up_weight[0], down_weight[0]),
    )
    parts = lax.all_to_all(parts, "kv", split_axis=0, concat_axis=0, tiled=True)
    head_values = merge_blocks(parts, value_up, ep_count, weights)
    all_values = lax.all_to_all(head_values, "ep", split_axis=0, concat_axis=0, tiled=True)
    own_rows = all_values.shape[0] // kv_count
    projected = project(all_values, out_proj, kv_count, weights)
    projected = lax.all_to_all(projected, "kv", split_axis=0, concat_axis=0, tiled=True)
    attended, spread = add_residual(projected, residual, kv_count * chips, weights)

    mine = lax.all_to_all(
        spread, both, split_axis=0, concat_axis=0, tiled=True, axis_index_groups=same_core
    )
    mine = regroup(mine, chips, weights)
    other = lax.ppermute(mine, "ep", other_core)
    keep, give = run_expert(
        mine,
        other,
        norm_gain[None],
        route_ids.T,
        route_gates.T,
        *weights,
    )
    given = lax.ppermute(give, "ep", other_core)
    summed = add_pair(keep, given, own_rows)
    arrived = lax.all_to_all(
        summed, both, split_axis=0, concat_axis=0, tiled=True, axis_index_groups=same_core
    )
    return (attended, add_total(arrived))


def solution(mesh):
    return jax.shard_map(
        on_device,
        mesh=mesh,
        in_specs=(
            P("ep", None, None),
            P("ep", "kv", None),
            P("ep"),
            P("kv", None, None),
            P("kv", "ep"),
            P("kv", "ep"),
            P(),
            P(),
            P(),
            P("kv", None, "ep"),
            P("kv", None, "ep"),
            P("kv", "ep", None),
        ),
        out_specs=(P("kv", "ep"), P("kv", "ep")),
        check_vma=False,
    )
```

```python
import functools

import jax
import jax.numpy as jnp
from jax import lax
from jax.experimental import pallas as pl
from jax.experimental.pallas import tpu as pltpu
from jax.sharding import PartitionSpec as P

SCORE_SCALE = 0.07216878364870323
LOG2_E = 1.4426950408889634
NEG_FILL = -1e30
NORM_EPS = 1e-06
LANES = 128
MIB = 1 << 20


def in_hbm(array):
    return pltpu.with_memory_space_constraint(array, pltpu.HBM)


def split_three(value):
    high = value.astype(jnp.bfloat16).astype(jnp.float32)
    rest = value - high
    mid = rest.astype(jnp.bfloat16).astype(jnp.float32)
    return high, mid, rest - mid


def attention_kernel(lengths_ref, q_hbm, cache_hbm, *refs):
    weight_count = (len(refs) - 4) // 2
    weights_hbm = refs[:weight_count]
    out_ref = refs[weight_count]
    weights_ref = refs[weight_count + 1 : -3]
    q_ref, cache_ref, arrived = refs[-3:]
    row_count, unused_width, ctx_len = cache_ref.shape
    head_count = q_ref.shape[2]
    groups = out_ref.shape[0]
    lat_width = out_ref.shape[2]
    per_group = head_count // groups
    start = lax.axis_index("kv") * ctx_len

    def fetch(row):
        return (
            pltpu.make_async_copy(q_hbm.at[row], q_ref.at[row], arrived.at[0, row]),
            pltpu.make_async_copy(cache_hbm.at[row], cache_ref.at[row], arrived.at[1, row]),
        )

    extra_copies = [
        pltpu.make_async_copy(weights_hbm[i], weights_ref[i], arrived.at[2, i])
        for i in range(weight_count)
    ]
    for row in range(row_count):
        for copy in fetch(row):
            copy.start()
    for copy in extra_copies:
        copy.start()
    position = lax.broadcasted_iota(jnp.int32, (head_count, ctx_len), 1)
    square = (head_count, head_count)
    same = lax.broadcasted_iota(jnp.int32, square, 0) == lax.broadcasted_iota(
        jnp.int32, square, 1
    )
    line = lax.broadcasted_iota(jnp.int32, (row_count, head_count), 0)
    levels = jnp.zeros((row_count, head_count), jnp.float32)
    for pair in range(0, row_count, 2):
        rows = (pair, pair + 1)
        for row in rows:
            for copy in fetch(row):
                copy.wait()
        scores = [
            lax.dot_general(
                q_ref[row],
                cache_ref[row],
                (((0,), (0,)), ((), ())),
                preferred_element_type=jnp.float32,
            )
            for row in rows
        ]
        scores = [
            jnp.where(position < lengths_ref[row] - start, s * (SCORE_SCALE * LOG2_E), NEG_FILL)
            for row, s in zip(rows, scores)
        ]
        tops = [jnp.max(s, axis=1, keepdims=True) for s in scores]
        terms = [jnp.exp2(s - top) for s, top in zip(scores, tops)]
        totals = [jnp.sum(t, axis=1, keepdims=True) for t in terms]
        outs = [
            lax.dot_general(
                t.astype(jnp.bfloat16),
                cache_ref[row, :lat_width, :],
                (((1,), (1,)), ((), ())),
                preferred_element_type=jnp.float32,
            )
            for row, t in zip(rows, terms)
        ]
        outs = [
            (o * (1.0 / total)).reshape(groups, per_group, lat_width)
            for o, total in zip(outs, totals)
        ]
        spot = slice(pair * per_group, (pair + 2) * per_group)
        out_ref[:, spot, :] = jnp.concatenate(outs, axis=1).astype(jnp.bfloat16)
        for row, top, total in zip(rows, tops, totals):
            level = jnp.sum(
                jnp.where(same, top + jnp.log2(total), 0.0), axis=0, keepdims=True
            )
            levels = jnp.where(line == row, level, levels)
    blank = jnp.zeros((row_count, lat_width - 3 * head_count), jnp.float32)
    stats = jnp.concatenate(split_three(levels) + (blank,), axis=1).astype(jnp.bfloat16)
    for k in range(groups):
        out_ref[k, row_count * per_group :, :] = stats
    for copy in extra_copies:
        copy.wait()


def attend_block(lengths, queries, latent_cache, groups, lat_width, weights):
    row_count, width, ctx_len = latent_cache.shape
    head_count = queries.shape[2]
    pairs = row_count * (head_count // groups)
    hbm = pl.BlockSpec(memory_space=pltpu.HBM)
    vmem = pl.BlockSpec(memory_space=pltpu.VMEM)
    return pl.pallas_call(
        attention_kernel,
        in_specs=[pl.BlockSpec(memory_space=pltpu.SMEM)] + [hbm] * (2 + len(weights)),
        out_specs=[vmem] * (1 + len(weights)),
        out_shape=[jax.ShapeDtypeStruct((groups, pairs + row_count, lat_width), jnp.bfloat16)]
        + [pltpu.VMEM(w.shape, w.dtype) for w in weights],
        scratch_shapes=[
            pltpu.VMEM((row_count, width, head_count), jnp.bfloat16),
            pltpu.VMEM((row_count, width, ctx_len), jnp.bfloat16),
            pltpu.SemaphoreType.DMA((3, row_count)),
        ],
        compiler_params=pltpu.CompilerParams(vmem_limit_bytes=28 * MIB),
        cost_estimate=pl.CostEstimate(
            flops=2 * row_count * head_count * ctx_len * (width + lat_width),
            bytes_accessed=2 * latent_cache.size + 2 * queries.size,
            transcendentals=row_count * head_count * ctx_len,
        ),
        name="attend_block",
    )(in_hbm(lengths), in_hbm(queries), in_hbm(latent_cache), *(in_hbm(w) for w in weights))


def merge_kernel(parts_ref, value_ref, *refs):
    out_ref, merged_ref = refs[-2:]
    block_count = parts_ref.shape[0]
    heads, lat_width, value_width = value_ref.shape
    rows = parts_ref.shape[1] // (heads + 1)
    pairs = rows * heads
    lanes = heads * block_count
    stats = parts_ref[:, pairs:, :].astype(jnp.float32)
    levels = (
        stats[:, :, :lanes] + stats[:, :, lanes : 2 * lanes] + stats[:, :, 2 * lanes : 3 * lanes]
    )
    factor = jnp.exp2(levels - jnp.max(levels, axis=0, keepdims=True))
    factor = factor / jnp.sum(factor, axis=0, keepdims=True)
    shape = (rows, heads, lanes)
    own = lax.broadcasted_iota(jnp.int32, shape, 2) == lax.broadcasted_iota(
        jnp.int32, shape, 1
    ) + heads * lax.axis_index("kv")
    merged = jnp.zeros((pairs, lat_width), jnp.float32)
    for k in range(block_count):
        column = jnp.sum(jnp.where(own, factor[k][:, None, :], 0.0), axis=2, keepdims=True)
        merged = merged + column.reshape(pairs, 1) * parts_ref[k, :pairs, :].astype(jnp.float32)
    tiles = merged_ref.shape[0]
    for t in range(tiles):
        merged_ref[t] = merged[:, t * LANES : (t + 1) * LANES]
    copies = out_ref.shape[0] // rows
    for h in range(heads):
        attention = jnp.concatenate(
            [merged_ref[t, pl.ds(h, rows, stride=heads), :] for t in range(tiles)], axis=1
        ).astype(jnp.bfloat16)
        value = jnp.dot(attention, value_ref[h], preferred_element_type=jnp.float32)
        out_ref[:, h * value_width : (h + 1) * value_width] = jnp.concatenate(
            [value] * copies, axis=0
        ).astype(jnp.bfloat16)


def merge_blocks(parts, value_up, copies, held):
    heads, lat_width, value_width = value_up.shape
    pairs = parts.shape[1] // (heads + 1) * heads
    return pl.pallas_call(
        merge_kernel,
        out_shape=jax.ShapeDtypeStruct(
            (copies * (pairs // heads), heads * value_width), jnp.bfloat16
        ),
        scratch_shapes=[pltpu.VMEM((lat_width // LANES, pairs, LANES), jnp.float32)],
        compiler_params=pltpu.CompilerParams(vmem_limit_bytes=12 * MIB),
        name="merge_blocks",
    )(parts, value_up, *held)


def project_kernel(values_ref, proj_ref, *refs):
    out_ref = refs[-1]
    own_rows = out_ref.shape[1]
    projected = jnp.dot(values_ref[...], proj_ref[...], preferred_element_type=jnp.float32)
    for k in range(out_ref.shape[0]):
        out_ref[k] = projected[k * own_rows : (k + 1) * own_rows].astype(jnp.bfloat16)


def project(values, proj, groups, held):
    rows = values.shape[0]
    cols = proj.shape[1]
    return pl.pallas_call(
        project_kernel,
        out_shape=jax.ShapeDtypeStruct((groups, rows // groups, cols), jnp.bfloat16),
        compiler_params=pltpu.CompilerParams(vmem_limit_bytes=12 * MIB),
        cost_estimate=pl.CostEstimate(
            flops=2 * rows * proj.size, bytes_accessed=2 * proj.size, transcendentals=0
        ),
        name="project",
    )(values, proj, *held)


def residual_kernel(parts_ref, residual_ref, *refs):
    attended_ref, spread_ref = refs[-2:]
    total = residual_ref[...].astype(jnp.float32)
    for k in range(parts_ref.shape[0]):
        total = total + parts_ref[k].astype(jnp.float32)
    attended = total.astype(jnp.bfloat16)
    attended_ref[...] = attended
    for i in range(spread_ref.shape[0]):
        spread_ref[i] = attended


def add_residual(parts, residual, copies, held):
    return pl.pallas_call(
        residual_kernel,
        out_shape=(
            pltpu.VMEM(residual.shape, jnp.bfloat16),
            jax.ShapeDtypeStruct((copies,) + residual.shape, jnp.bfloat16),
        ),
        compiler_params=pltpu.CompilerParams(vmem_limit_bytes=8 * MIB),
        cost_estimate=pl.CostEstimate(
            flops=parts.size, bytes_accessed=2 * copies * residual.size, transcendentals=0
        ),
        name="add_residual",
    )(parts, residual, *held)


def half_product(parts_ref, gain_ref, w_gate_ref, w_up_ref, core):
    col_count = parts_ref.shape[2]
    chips = gain_ref.shape[1] // (2 * col_count)
    each = parts_ref.shape[0] // chips
    row_count = each * parts_ref.shape[1]
    squares = jnp.zeros((row_count, col_count), jnp.float32)
    gate_act = jnp.zeros((row_count, w_gate_ref.shape[1]), jnp.float32)
    up_act = gate_act
    for y in range(chips):
        at = pl.ds(pl.multiple_of((2 * y + core) * col_count, LANES), col_count)
        wide = jnp.concatenate(
            [parts_ref[y * each + k].astype(jnp.float32) for k in range(each)], axis=0
        )
        squares = squares + wide * wide
        scaled = (wide * gain_ref[:, at]).astype(jnp.bfloat16)
        gate_act = gate_act + jnp.dot(
            scaled, w_gate_ref[at, :], preferred_element_type=jnp.float32
        )
        up_act = up_act + jnp.dot(scaled, w_up_ref[at, :], preferred_element_type=jnp.float32)
    return gate_act, up_act, jnp.sum(squares, axis=1, keepdims=True)


def own_half_kernel(mine_ref, gain_ref, w_gate_ref, w_up_ref, *refs):
    gate_ref, up_ref, squares_ref = refs[-3:]
    core = lax.rem(lax.axis_index("ep"), 2)
    gate_act, up_act, squares = half_product(mine_ref, gain_ref, w_gate_ref, w_up_ref, core)
    gate_ref[...] = gate_act
    up_ref[...] = up_act
    squares_ref[...] = jnp.broadcast_to(squares, squares_ref.shape)


def run_own_half(mine, gain, w_gate, w_up, held):
    row_count = mine.shape[0] * mine.shape[1] * 2 * mine.shape[2] // w_gate.shape[0]
    width = w_gate.shape[1]
    return pl.pallas_call(
        own_half_kernel,
        out_shape=(
            jax.ShapeDtypeStruct((row_count, width), jnp.float32),
            jax.ShapeDtypeStruct((row_count, width), jnp.float32),
            jax.ShapeDtypeStruct((row_count, LANES), jnp.float32),
        ),
        compiler_params=pltpu.CompilerParams(vmem_limit_bytes=12 * MIB),
        cost_estimate=pl.CostEstimate(
            flops=2 * row_count * w_gate.size, bytes_accessed=2 * w_gate.size, transcendentals=0
        ),
        name="own_half",
    )(mine, gain, w_gate, w_up, *held)


def expert_kernel(
    other_ref,
    gate_ref,
    up_ref,
    squares_ref,
    gain_ref,
    ids_ref,
    gates_ref,
    w_gate_ref,
    w_up_ref,
    w_down_ref,
    attended_ref,
    give_ref,
    hidden_ref,
    share_ref,
    attended_hbm,
    sent,
):
    save = pltpu.make_async_copy(attended_ref, attended_hbm, sent)
    save.start()
    chips, row_count, col_count = give_ref.shape
    full_width = gain_ref.shape[1]
    expert = lax.axis_index("kv")
    other = 1 - lax.rem(lax.axis_index("ep"), 2)
    gate_act, up_act, squares = half_product(other_ref, gain_ref, w_gate_ref, w_up_ref, other)
    squares = squares + squares_ref[:, :1]
    inverse = lax.rsqrt(squares / full_width + NORM_EPS)
    gate_act = (gate_act + gate_ref[...]) * inverse
    up_act = (up_act + up_ref[...]) * inverse
    hidden = (gate_act / (1.0 + jnp.exp(-gate_act)) * up_act).astype(jnp.bfloat16)
    hidden_ref[...] = hidden
    chosen = jnp.where(ids_ref[...] == expert, gates_ref[...], 0.0)
    in_lanes = jnp.sum(chosen, axis=0, keepdims=True)
    square = (row_count, row_count)
    same = lax.broadcasted_iota(jnp.int32, square, 0) == lax.broadcasted_iota(
        jnp.int32, square, 1
    )
    row_gate = jnp.sum(jnp.where(same, in_lanes, 0.0), axis=1, keepdims=True)
    share_ref[...] = jnp.broadcast_to(row_gate, share_ref.shape)
    for y in range(chips):
        at = pl.ds(pl.multiple_of((2 * y + other) * col_count, LANES), col_count)
        terms = jnp.dot(hidden, w_down_ref[:, at], preferred_element_type=jnp.float32)
        give_ref[y] = (terms * row_gate).astype(jnp.bfloat16)
    save.wait()


def run_expert(other, gate, up, squares, gain, ids, gates, w_gate, w_up, w_down, attended):
    row_count, hidden_width = gate.shape
    full_width = w_gate.shape[0]
    chips = full_width // (2 * other.shape[2])
    vmem = pl.BlockSpec(memory_space=pltpu.VMEM)
    return pl.pallas_call(
        expert_kernel,
        in_specs=[vmem] * 11,
        out_specs=(vmem, vmem, vmem, pl.BlockSpec(memory_space=pltpu.HBM)),
        out_shape=(
            jax.ShapeDtypeStruct((chips, row_count, other.shape[2]), jnp.bfloat16),
            jax.ShapeDtypeStruct((row_count, hidden_width), jnp.bfloat16),
            jax.ShapeDtypeStruct((row_count, LANES), jnp.float32),
            jax.ShapeDtypeStruct(attended.shape, attended.dtype),
        ),
        scratch_shapes=[pltpu.SemaphoreType.DMA],
        compiler_params=pltpu.CompilerParams(vmem_limit_bytes=12 * MIB),
        cost_estimate=pl.CostEstimate(
            flops=4 * row_count * full_width * hidden_width,
            bytes_accessed=4 * full_width * hidden_width,
            transcendentals=row_count * hidden_width,
        ),
        name="run_expert",
    )(other, gate, up, squares, gain, ids, gates, w_gate, w_up, w_down, attended)


def keep_kernel(hidden_ref, share_ref, w_down_ref, keep_ref):
    chips, unused_rows, col_count = keep_ref.shape
    core = lax.rem(lax.axis_index("ep"), 2)
    hidden = hidden_ref[...]
    row_gate = share_ref[:, :1]
    for y in range(chips):
        at = pl.ds(pl.multiple_of((2 * y + core) * col_count, LANES), col_count)
        terms = jnp.dot(hidden, w_down_ref[:, at], preferred_element_type=jnp.float32)
        keep_ref[y] = (terms * row_gate).astype(jnp.bfloat16)


def run_keep(hidden, share, w_down, like):
    return pl.pallas_call(
        keep_kernel,
        out_shape=jax.ShapeDtypeStruct(like.shape, like.dtype),
        compiler_params=pltpu.CompilerParams(vmem_limit_bytes=12 * MIB),
        cost_estimate=pl.CostEstimate(
            flops=hidden.shape[0] * w_down.size, bytes_accessed=w_down.size, transcendentals=0
        ),
        name="run_keep",
    )(hidden, share, w_down)


def pair_kernel(keep_ref, given_ref, out_ref):
    chips, row_count, unused_cols = keep_ref.shape
    own_rows = out_ref.shape[1]
    for y in range(chips):
        both = keep_ref[y].astype(jnp.float32) + given_ref[y].astype(jnp.float32)
        for k in range(row_count // own_rows):
            out_ref[y * (row_count // own_rows) + k] = both[
                k * own_rows : (k + 1) * own_rows
            ].astype(jnp.bfloat16)


def add_pair(keep, given, own_rows):
    chips, row_count, col_count = keep.shape
    return pl.pallas_call(
        pair_kernel,
        out_shape=jax.ShapeDtypeStruct(
            (chips * row_count // own_rows, own_rows, col_count), jnp.bfloat16
        ),
        compiler_params=pltpu.CompilerParams(vmem_limit_bytes=8 * MIB),
        cost_estimate=pl.CostEstimate(
            flops=keep.size, bytes_accessed=6 * keep.size, transcendentals=0
        ),
        name="add_pair",
    )(keep, given)


def total_kernel(parts_ref, out_ref):
    total = parts_ref[0].astype(jnp.float32)
    for k in range(1, parts_ref.shape[0]):
        total = total + parts_ref[k].astype(jnp.float32)
    out_ref[...] = total.astype(jnp.bfloat16)


def add_total(parts):
    return pl.pallas_call(
        total_kernel,
        out_shape=jax.ShapeDtypeStruct(parts.shape[1:], jnp.bfloat16),
        compiler_params=pltpu.CompilerParams(vmem_limit_bytes=8 * MIB),
        name="add_total",
    )(parts)


def on_device(
    queries,
    latent_cache,
    lengths,
    value_up,
    out_proj,
    residual,
    norm_gain,
    route_ids,
    route_gates,
    gate_weight,
    up_weight,
    down_weight,
):
    kv_count = lax.axis_size("kv")
    ep_count = lax.axis_size("ep")
    chips = ep_count // 2
    both = ("kv", "ep")
    same_core = [
        [kv * ep_count + y * 2 + c for y in range(chips) for kv in range(kv_count)]
        for c in range(2)
    ]
    other_core = [(i, i ^ 1) for i in range(ep_count)]
    lat_width = value_up.shape[1]

    parts, *weights = attend_block(
        lengths,
        jnp.swapaxes(queries, 1, 2),
        jnp.swapaxes(latent_cache, 1, 2),
        kv_count,
        lat_width,
        (gate_weight[0], up_weight[0], down_weight[0]),
    )
    parts = lax.all_to_all(parts, "kv", split_axis=0, concat_axis=0, tiled=True)
    head_values = merge_blocks(parts, value_up, ep_count, weights)
    all_values = lax.all_to_all(head_values, "ep", split_axis=0, concat_axis=0, tiled=True)
    own_rows = all_values.shape[0] // kv_count
    projected = project(all_values, out_proj, kv_count, weights)
    projected = lax.all_to_all(projected, "kv", split_axis=0, concat_axis=0, tiled=True)
    attended, spread = add_residual(projected, residual, kv_count * chips, weights)

    mine = lax.all_to_all(
        spread, both, split_axis=0, concat_axis=0, tiled=True, axis_index_groups=same_core
    )
    other = lax.ppermute(mine, "ep", other_core)
    gain = norm_gain[None]
    w_gate, w_up, w_down = weights
    partial = run_own_half(mine, gain, w_gate, w_up, [w_down])
    give, hidden, share, attended = run_expert(
        other, *partial, gain, route_ids.T, route_gates.T, w_gate, w_up, w_down, attended
    )
    given = lax.ppermute(give, "ep", other_core)
    keep = run_keep(hidden, share, w_down, give)
    summed = add_pair(keep, given, own_rows)
    arrived = lax.all_to_all(
        summed, both, split_axis=0, concat_axis=0, tiled=True, axis_index_groups=same_core
    )
    return (attended, add_total(arrived))


def solution(mesh):
    return jax.shard_map(
        on_device,
        mesh=mesh,
        in_specs=(
            P("ep", None, None),
            P("ep", "kv", None),
            P("ep"),
            P("kv", None, None),
            P("kv", "ep"),
            P("kv", "ep"),
            P(),
            P(),
            P(),
            P("kv", None, "ep"),
            P("kv", None, "ep"),
            P("kv", "ep", None),
        ),
        out_specs=(P("kv", "ep"), P("kv", "ep")),
        check_vma=False,
    )
```
